32 devices in a mesh: groups: 2 (over y), expert: 8 (over z, core), dp: 2 (over x).
Axes of the slice: x: 2, y: 2, z: 4, core: 2. Of those that a mesh axis runs over, the one named last changes fastest.
Arguments:
- tokens: bfloat16 [768, 2048], P(('groups', 'expert', 'dp')), parts along dimension 0, may hold values from -6 to 6
- cotangent: bfloat16 [768, 2048], P(('groups', 'expert', 'dp')), parts along dimension 0, may hold values from -6 to 6
- routes: int32 [768, 6], P(('groups', 'expert', 'dp')), parts along dimension 0, may hold values from 0 to 15, all different within a row; in each aligned block of 24 rows (0 to 23, 24 to 47, ...) at most 11 rows name the same one
- mix_weights: bfloat16 [768, 6], P(('groups', 'expert', 'dp')), parts along dimension 0, may hold values from 0.049804688 to 0.5
- gate_matrix: bfloat16 [2048, 16384], P(None, ('expert', 'dp')), may hold values from -0.125 to 0.125
- up_matrix: bfloat16 [2048, 16384], P(None, ('expert', 'dp')), may hold values from -0.125 to 0.125
- down_matrix: bfloat16 [16384, 2048], P(('expert', 'dp')), may hold values from -0.1875 to 0.1875
Outputs:
- grad_tokens: bfloat16 [768, 2048], P(('groups', 'expert', 'dp')), parts along dimension 0
- grad_mix: float32 [768, 6], P(('groups', 'expert', 'dp')), parts along dimension 0
- grad_gate: float32 [2048, 32768], P(None, ('groups', 'expert', 'dp')), parts along dimension 1
- grad_up: float32 [2048, 32768], P(None, ('groups', 'expert', 'dp')), parts along dimension 1
- grad_down: float32 [32768, 2048], P(('groups', 'expert', 'dp')), parts along dimension 0
The draws below stay inside these ranges and needn't reach their ends.
There are 2 independent parts, one for each index of `groups`. The reference program is written for one: setup_inputs(seed, part) draws one part's arguments, and reference() takes and returns one part's arrays. A program takes and returns all parts, laid end to end along the dimension named above; an argument that names none is the same for every part. Nothing has to cross between parts.
Inputs may be any that keep to these rules, and one draw needn't show every extreme that they name: `routes`: each row names 6 different experts. In each aligned block of 24 rows (the tokens of one device) no expert is named more than 11 times, a bound that some block reaches.
All inputs are finite; a program needn't handle non-finite values.
Results may differ from the reference program's by a relative error of at most 0.0085.
Values may be sent and summed in bfloat16 or wider, within the bound.
A program may use at most 128 MiB of HBM per device.

```python
import math
import jax
import jax.numpy as jnp
import numpy as np
from jax import lax

D = 2048
FF = 1024
TOP = 6
TOK_DEV = 24
EXPERTS = 16
MOST = 11
HID_DEV = 1024
TOKENS = 384
N_EXPERT = 8
N_DP = 2


def shard_levels(stream_key, shape, split, least, top_value):
    def one(position, parts):
        steps = jax.random.uniform(jax.random.fold_in(jax.random.fold_in(stream_key, 6), position), (parts,), jnp.float32, least / len(split), top_value / len(split))
        return jnp.repeat(jnp.exp(steps), shape[position] // parts).reshape((-1,) + (1,) * (len(shape) - position - 1))

    gain = one(*split[0])
    for cut in split[1:]:
        gain = gain * one(*cut)
    return gain


def assign_block(stream_key, own, number, rows, count, top, bound, lean):
    sequence = jax.random.permutation(stream_key, count)
    crowded, usual = load_shares(count, rows * top, bound, lean, True), load_shares(count, rows * top, bound, lean, False)
    places = jnp.arange(count)

    def named(sizes, rotation):
        used = int((sizes > 0).sum())
        fixed = max(1, used // 4)
        passed = fixed + (places - fixed + rotation * (used - fixed)) % max(1, count - fixed)
        return jnp.zeros((count,), jnp.int32).at[sequence[jnp.where(places < fixed, places, passed)]].set(jnp.asarray(sizes, jnp.int32))

    sizes = jnp.where(number % 4 == 0, named(crowded, number // 4), named(usual, number - number // 4 - 1))
    mixed = jax.random.permutation(jax.random.fold_in(own, 3), count)
    source_of, sink = mixed[0:count // 2 * 2:2], mixed[1:count // 2 * 2:2]
    margin = jnp.minimum(sizes[source_of] - 1, bound - sizes[sink]) // 2
    margin = jnp.where((source_of == sequence[0]) | (sink == sequence[0]) | (sizes[sink] == 0), 0, jnp.maximum(margin, 0))
    passed = jax.random.randint(jax.random.fold_in(own, 4), (count // 2,), 0, 1 << 20) % (margin + 1)
    sizes = sizes.at[source_of].add(-passed).at[sink].add(passed)
    members = jnp.searchsorted(jnp.cumsum(sizes), jnp.arange(rows * top), side="right").astype(jnp.int32)
    grid = members.reshape(top, rows).T
    grid = grid[jax.random.permutation(jax.random.fold_in(own, 1), rows)]
    rotation = jax.random.randint(jax.random.fold_in(own, 2), (rows, 1), 0, top)
    return jnp.take_along_axis(grid, (jnp.arange(top)[None, :] + rotation) % top, axis=1)


def load_shares(amount, total, bound, lean, full):
    weights = [(1 << 20) // math.isqrt(standing ** lean) + 1 for standing in range(1, amount + 1)]
    largest = bound if full else min(bound, max(-(-total // amount), total * weights[0] // sum(weights)))
    least = 1 if total - largest >= amount - 1 else 0
    given, spare = [largest] + [least] * (amount - 1), total - largest - least * (amount - 1)
    while spare > 0:
        candidates = [i for i in range(1, amount) if given[i] < largest] or [i for i in range(1, amount) if given[i] < bound]
        whole, budget = sum([weights[i] for i in candidates]), spare
        for i in candidates:
            extra = min(bound - given[i], max(1, budget * weights[i] // whole), spare)
            given[i] = given[i] + extra
            spare = spare - extra
    return np.array(given)


def normal_values(own_key, extent, spread, limit, shards=(), held_as=jnp.bfloat16):
    drawn = spread * jax.random.normal(own_key, extent, jnp.float32)
    if shards:
        drawn = drawn * shard_levels(own_key, extent, shards, -0.22, 0.18)
    return jnp.clip(drawn, -limit, limit).astype(held_as)


def setup_inputs(seed: int = 0, part: int = 0) -> dict:
    keys = jax.random.split(jax.random.key(seed), 8)
    own_keys = jax.random.split(jax.random.fold_in(keys[7], part), 8)
    tokens = normal_values(own_keys[0], (TOKENS, D), 1.0, 6.0, ((0, 16),))
    cotangent = normal_values(own_keys[1], (TOKENS, D), 1.0, 6.0, ((0, 16),))
    routes_keys = jax.random.split(jax.random.fold_in(own_keys[2], 1), TOKENS // TOK_DEV)
    routes_turns = jax.random.permutation(jax.random.fold_in(own_keys[2], 3), TOKENS // TOK_DEV)
    routes = jax.vmap(lambda own, number: assign_block(jax.random.fold_in(own_keys[2], 2), own, number, TOK_DEV, EXPERTS, TOP, MOST, 2))(routes_keys, routes_turns).reshape((TOKENS, TOP))
    mix_weights = jnp.clip(jnp.exp(math.log(0.5) - 2.306499 * jax.random.uniform(own_keys[3], (TOKENS, TOP), jnp.float32) ** shard_levels(own_keys[3], (TOKENS, TOP), ((0, 16),), -0.2, 0.2)), 0.049804688, 0.5).astype(jnp.bfloat16)
    gate_matrix = normal_values(keys[4], (D, EXPERTS * FF), D ** -0.5, 0.125, ((1, 16),))
    up_matrix = normal_values(keys[5], (D, EXPERTS * FF), D ** -0.5, 0.125, ((1, 16),))
    down_matrix = normal_values(keys[6], (EXPERTS * FF, D), FF ** -0.5, 0.1875, ((0, 16),))
    return {"tokens": tokens, "cotangent": cotangent, "routes": routes, "mix_weights": mix_weights, "gate_matrix": gate_matrix, "up_matrix": up_matrix, "down_matrix": down_matrix}


def reference(tokens, cotangent, routes, mix_weights, gate_matrix, up_matrix, down_matrix):
    row_total = TOKENS * TOP
    capacity = MOST * N_EXPERT * N_DP
    blocks = FF // HID_DEV
    expert_ids = routes.reshape(row_total).astype(jnp.int32)
    order = jnp.argsort(expert_ids, stable=True).astype(jnp.int32)
    expert_range = jnp.arange(EXPERTS, dtype=jnp.int32)
    counts = jnp.sum((expert_ids[:, None] == expert_range[None, :]).astype(jnp.int32), axis=0).astype(jnp.int32)
    starts = (jnp.cumsum(counts) - counts).astype(jnp.int32)
    padded = jnp.concatenate([order, jnp.full((capacity,), row_total, jnp.int32)])
    mix_flat = jnp.concatenate([mix_weights.reshape(row_total).astype(jnp.float32), jnp.zeros((1,), jnp.float32)])

    def expert_step(carry, expert):
        grad_rows, mix_rows = carry
        index = lax.dynamic_slice(padded, (starts[expert].astype(jnp.int32),), (capacity,))
        valid = jnp.arange(capacity, dtype=jnp.int32) < counts[expert]
        index = jnp.where(valid, index, jnp.int32(row_total)).astype(jnp.int32)
        token_index = jnp.minimum(index // TOP, TOKENS - 1).astype(jnp.int32)
        row_tokens = jnp.where(valid[:, None], tokens[token_index], jnp.zeros((), tokens.dtype))
        row_cotan = jnp.where(valid[:, None], cotangent[token_index], jnp.zeros((), cotangent.dtype))
        mix_column = mix_flat[index][:, None]
        start = (expert * FF).astype(jnp.int32)
        zero = jnp.int32(0)
        gate_cols = lax.dynamic_slice(gate_matrix, (zero, start), (D, FF))
        up_cols = lax.dynamic_slice(up_matrix, (zero, start), (D, FF))
        down_rows = lax.dynamic_slice(down_matrix, (start, zero), (FF, D))
        pre_gate = jnp.dot(row_tokens, gate_cols, preferred_element_type=jnp.float32)
        pre_up = jnp.dot(row_tokens, up_cols, preferred_element_type=jnp.float32)
        sigmoid_gate = jax.nn.sigmoid(pre_gate)
        activated = pre_gate * sigmoid_gate
        hidden = (activated * pre_up).astype(jnp.bfloat16)
        back_hidden = jnp.dot(row_cotan, down_rows.T, preferred_element_type=jnp.float32)
        scaled_cotan = (mix_column * row_cotan.astype(jnp.float32)).astype(jnp.bfloat16)
        grad_hidden = mix_column * back_hidden
        grad_upper = (grad_hidden * activated).astype(jnp.bfloat16)
        grad_pregate = (grad_hidden * pre_up * sigmoid_gate * (1.0 + pre_gate * (1.0 - sigmoid_gate))).astype(jnp.bfloat16)
        down_grad = jnp.dot(hidden.T, scaled_cotan, preferred_element_type=jnp.float32)
        gate_grad = jnp.dot(row_tokens.T, grad_pregate, preferred_element_type=jnp.float32)
        up_grad = jnp.dot(row_tokens.T, grad_upper, preferred_element_type=jnp.float32)
        partial_value = jnp.einsum("rgh,dgh->rgd", grad_pregate.reshape(capacity, blocks, HID_DEV).astype(jnp.float32), gate_cols.reshape(D, blocks, HID_DEV).astype(jnp.float32))
        partial_value = partial_value + jnp.einsum("rgh,dgh->rgd", grad_upper.reshape(capacity, blocks, HID_DEV).astype(jnp.float32), up_cols.reshape(D, blocks, HID_DEV).astype(jnp.float32))
        partial_value = lax.optimization_barrier(partial_value.astype(jnp.bfloat16)).astype(jnp.float32).sum(axis=1)
        mix_part = (hidden.astype(jnp.float32) * back_hidden).reshape(capacity, blocks, HID_DEV).sum(axis=2)
        mix_part = lax.optimization_barrier(mix_part.astype(jnp.bfloat16)).astype(jnp.float32).sum(axis=1)
        grad_rows = grad_rows.at[index].add(partial_value)
        mix_rows = mix_rows.at[index].add(mix_part)
        return (grad_rows, mix_rows), (gate_grad, up_grad, down_grad)

    start_carry = (jnp.zeros((row_total + 1, D), jnp.float32), jnp.zeros((row_total + 1,), jnp.float32))
    (grad_rows, mix_rows), (gate_all, up_all, down_all) = lax.scan(expert_step, start_carry, jnp.arange(EXPERTS, dtype=jnp.int32))
    grad_tokens = grad_rows[:row_total].reshape(TOKENS, TOP, D).sum(axis=1).astype(jnp.bfloat16)
    grad_mix = mix_rows[:row_total].reshape(TOKENS, TOP)
    grad_gate = jnp.transpose(gate_all, (1, 0, 2)).reshape(D, EXPERTS * FF)
    grad_up = jnp.transpose(up_all, (1, 0, 2)).reshape(D, EXPERTS * FF)
    grad_down = down_all.reshape(EXPERTS * FF, D)
    return (grad_tokens, grad_mix, grad_gate, grad_up, grad_down)
```

```python
import jax
import jax.numpy as jnp
from jax import lax
from jax.sharding import PartitionSpec as P


def expert_backward(row_tokens, row_cotan, row_mix, gate_matrix, up_matrix, down_matrix):
    contract_last = (((1,), (1,)), ((), ()))
    contract_first = (((0,), (0,)), ((), ()))
    pre_gate = jnp.dot(row_tokens, gate_matrix, preferred_element_type=jnp.float32)
    pre_up = jnp.dot(row_tokens, up_matrix, preferred_element_type=jnp.float32)
    sigmoid_gate = jax.nn.sigmoid(pre_gate)
    activated = pre_gate * sigmoid_gate
    hidden = (activated * pre_up).astype(jnp.bfloat16)
    back_hidden = lax.dot_general(
        row_cotan, down_matrix, contract_last, preferred_element_type=jnp.float32
    )
    mix_column = row_mix.astype(jnp.float32)[:, None]
    scaled_cotan = (mix_column * row_cotan.astype(jnp.float32)).astype(jnp.bfloat16)
    grad_hidden = mix_column * back_hidden
    grad_upper = (grad_hidden * activated).astype(jnp.bfloat16)
    grad_pregate = (
        grad_hidden * pre_up * sigmoid_gate * (1.0 + pre_gate * (1.0 - sigmoid_gate))
    ).astype(jnp.bfloat16)
    mix_partial = jnp.sum(hidden.astype(jnp.float32) * back_hidden, axis=1).astype(jnp.bfloat16)
    down_grad = lax.dot_general(
        hidden, scaled_cotan, contract_first, preferred_element_type=jnp.float32
    )
    gate_grad = lax.dot_general(
        row_tokens, grad_pregate, contract_first, preferred_element_type=jnp.float32
    )
    up_grad = lax.dot_general(
        row_tokens, grad_upper, contract_first, preferred_element_type=jnp.float32
    )
    joined_grad = jnp.concatenate([grad_pregate, grad_upper], axis=1)
    joined_weight = jnp.concatenate([gate_matrix, up_matrix], axis=1)
    token_partial = lax.dot_general(
        joined_grad, joined_weight, contract_last, preferred_element_type=jnp.float32
    ).astype(jnp.bfloat16)
    return (token_partial, mix_partial, gate_grad, up_grad, down_grad)


def local_exchange(tokens, cotangent, routes, mix_weights, gate_matrix, up_matrix, down_matrix):
    tok_count, features = tokens.shape
    top_count = routes.shape[1]
    columns = lax.axis_size("expert")
    dp_size = lax.axis_size("dp")
    team_size = dp_size // 2
    experts = 2 * columns
    slot_most = min(5 * tok_count * top_count // (4 * experts), tok_count)
    row_count = tok_count * top_count
    slot_count = experts * slot_most
    expert_ids = routes.reshape(row_count)
    onehot = (expert_ids[:, None] == jnp.arange(experts, dtype=jnp.int32)[None, :]).astype(
        jnp.bfloat16
    )
    row_index = jnp.arange(row_count, dtype=jnp.int32)
    earlier = (row_index[None, :] < row_index[:, None]).astype(jnp.bfloat16)
    prior_count = jnp.dot(earlier, onehot, preferred_element_type=jnp.float32)
    position = jnp.sum(prior_count * onehot.astype(jnp.float32), axis=1).astype(jnp.int32)
    slot_ids = expert_ids * slot_most + position
    slot_pick = (slot_ids[:, None] == jnp.arange(slot_count, dtype=jnp.int32)[None, :]).astype(
        jnp.bfloat16
    )
    token_rows = jnp.repeat(tokens, top_count, axis=0)
    cotan_rows = jnp.repeat(cotangent, top_count, axis=0)
    mix_rows = mix_weights.reshape(row_count, 1)
    pick_form = "rs,rd->sd"
    token_slots = jnp.einsum(
        pick_form, slot_pick, token_rows, preferred_element_type=jnp.float32
    ).astype(jnp.bfloat16)
    cotan_slots = jnp.einsum(
        pick_form, slot_pick, cotan_rows, preferred_element_type=jnp.float32
    ).astype(jnp.bfloat16)
    mix_slots = (
        jnp.einsum(pick_form, slot_pick, mix_rows, preferred_element_type=jnp.float32)
        .astype(jnp.bfloat16)
        .reshape(slot_count)
    )

    def spread(values):
        rest = values.shape[1:]
        lead = values.reshape((columns, 2, 1, slot_most) + rest)
        wide = jnp.broadcast_to(lead, (columns, 2, team_size, slot_most) + rest)
        return wide.reshape((columns, dp_size, slot_most) + rest)

    arrived = (
        lax.all_to_all(
            lax.all_to_all(spread(token_slots), "expert", split_axis=0, concat_axis=0, tiled=True),
            "dp",
            split_axis=1,
            concat_axis=1,
            tiled=True,
        ),
        lax.all_to_all(
            lax.all_to_all(spread(cotan_slots), "expert", split_axis=0, concat_axis=0, tiled=True),
            "dp",
            split_axis=1,
            concat_axis=1,
            tiled=True,
        ),
        lax.all_to_all(
            lax.all_to_all(spread(mix_slots), "expert", split_axis=0, concat_axis=0, tiled=True),
            "dp",
            split_axis=1,
            concat_axis=1,
            tiled=True,
        ),
    )
    token_partial, mix_partial, gate_grad, up_grad, down_grad = expert_backward(
        arrived[0].reshape(-1, features),
        arrived[1].reshape(-1, features),
        arrived[2].reshape(-1),
        gate_matrix,
        up_matrix,
        down_matrix,
    )
    returned = (
        lax.all_to_all(
            lax.all_to_all(
                token_partial.reshape(columns, dp_size, slot_most, features),
                "expert",
                split_axis=0,
                concat_axis=0,
                tiled=True,
            ),
            "dp",
            split_axis=1,
            concat_axis=1,
            tiled=True,
        ),
        lax.all_to_all(
            lax.all_to_all(
                mix_partial.reshape(columns, dp_size, slot_most),
                "expert",
                split_axis=0,
                concat_axis=0,
                tiled=True,
            ),
            "dp",
            split_axis=1,
            concat_axis=1,
            tiled=True,
        ),
    )
    token_sums = (
        returned[0]
        .reshape(columns, 2, team_size, slot_most, features)
        .astype(jnp.float32)
        .sum(axis=2)
        .reshape(slot_count, features)
    )
    mix_sums = (
        returned[1]
        .reshape(columns, 2, team_size, slot_most)
        .astype(jnp.float32)
        .sum(axis=2)
        .reshape(slot_count)
    )
    token_pick = slot_pick.reshape(tok_count, top_count, slot_count).astype(jnp.float32).sum(axis=1)
    grad_tokens = jnp.dot(token_pick, token_sums, precision=lax.Precision.HIGHEST).astype(
        jnp.bfloat16
    )
    grad_mix = jnp.dot(
        slot_pick.astype(jnp.float32), mix_sums[:, None], precision=lax.Precision.HIGHEST
    ).reshape(tok_count, top_count)
    return (grad_tokens, grad_mix, gate_grad, up_grad, down_grad)


def local_gather(tokens, cotangent, routes, mix_weights, gate_matrix, up_matrix, down_matrix):
    axes = ("expert", "dp")
    f32, bf16 = jnp.float32, jnp.bfloat16
    tok_count, features = tokens.shape
    top_count = routes.shape[1]
    devices = lax.axis_size("expert") * lax.axis_size("dp")
    experts = devices
    slot_most = min(5 * tok_count * top_count // (4 * experts), tok_count)
    rows = devices * slot_most
    mine = lax.axis_index("expert") * lax.axis_size("dp") + lax.axis_index("dp")
    extra = jnp.zeros((tok_count, 128 - 2 * top_count), bf16)
    packed = jnp.concatenate(
        [tokens, cotangent, routes.astype(bf16), mix_weights, extra], axis=1
    )
    world = lax.all_gather(packed, axes, axis=0, tiled=True)
    total = devices * tok_count
    tail = 2 * features
    named = world[:, tail : tail + top_count] == mine.astype(bf16)
    weight = jnp.sum(
        jnp.where(named, world[:, tail + top_count : tail + 2 * top_count], 0).astype(f32), axis=1
    )
    hit = jnp.any(named, axis=1).reshape(devices, tok_count)
    ahead = (
        jnp.arange(tok_count)[:, None] < jnp.arange(tok_count)[None, :]
    ).astype(bf16)
    place = jnp.dot(hit.astype(bf16), ahead, preferred_element_type=f32).astype(jnp.int32)
    place = place + jnp.arange(devices, dtype=jnp.int32)[:, None] * slot_most
    place = jnp.where(hit, place, -1).reshape(total)
    pick = (jnp.arange(rows, dtype=jnp.int32)[:, None] == place[None, :]).astype(bf16)
    row_both = jnp.dot(pick, world[:, :tail], preferred_element_type=f32).astype(bf16)
    row_mix = jnp.sum(pick.astype(f32) * weight[None, :], axis=1).astype(bf16)
    token_partial, mix_partial, gate_grad, up_grad, down_grad = expert_backward(
        row_both[:, :features], row_both[:, features:], row_mix, gate_matrix, up_matrix, down_matrix
    )
    lane = (jnp.arange(128, dtype=jnp.int32)[None, :] == mine).astype(bf16)
    back = jnp.concatenate([token_partial, mix_partial[:, None] * lane], axis=1)
    spread = lax.dot_general(
        pick, back, (((0,), (0,)), ((), ())), preferred_element_type=f32
    ).astype(bf16)
    home = lax.psum_scatter(spread, axes, scatter_dimension=0, tiled=True)
    grad_tokens = home[:, :features]
    chosen = routes[:, :, None] == jnp.arange(experts, dtype=jnp.int32)[None, None, :]
    grad_mix = jnp.sum(
        jnp.where(chosen, home[:, None, features : features + experts].astype(f32), 0.0), axis=2
    )
    return (grad_tokens, grad_mix, gate_grad, up_grad, down_grad)


def solution(mesh):
    local = local_gather if mesh.shape["dp"] == 2 else local_exchange
    in_specs = (
        P(("groups", "expert", "dp"), None),
        P(("groups", "expert", "dp"), None),
        P(("groups", "expert", "dp"), None),
        P(("groups", "expert", "dp"), None),
        P(None, ("expert", "dp")),
        P(None, ("expert", "dp")),
        P(("expert", "dp"), None),
    )
    out_specs = (
        P(("groups", "expert", "dp"), None),
        P(("groups", "expert", "dp"), None),
        P(None, ("groups", "expert", "dp")),
        P(None, ("groups", "expert", "dp")),
        P(("groups", "expert", "dp"), None),
    )
    return jax.shard_map(local, mesh=mesh, in_specs=in_specs, out_specs=out_specs, check_vma=False)
```

```python
import jax
import jax.numpy as jnp
from jax import lax
from jax.experimental import pallas as pl
from jax.experimental.pallas import tpu as pltpu
from jax.sharding import PartitionSpec as P


def expert_backward(row_tokens, row_cotan, row_mix, gate_matrix, up_matrix, down_matrix):
    contract_last = (((1,), (1,)), ((), ()))
    contract_first = (((0,), (0,)), ((), ()))
    pre_gate = jnp.dot(row_tokens, gate_matrix, preferred_element_type=jnp.float32)
    pre_up = jnp.dot(row_tokens, up_matrix, preferred_element_type=jnp.float32)
    sigmoid_gate = jax.nn.sigmoid(pre_gate)
    activated = pre_gate * sigmoid_gate
    hidden = (activated * pre_up).astype(jnp.bfloat16)
    back_hidden = lax.dot_general(
        row_cotan, down_matrix, contract_last, preferred_element_type=jnp.float32
    )
    mix_column = row_mix.astype(jnp.float32)[:, None]
    scaled_cotan = (mix_column * row_cotan.astype(jnp.float32)).astype(jnp.bfloat16)
    grad_hidden = mix_column * back_hidden
    grad_upper = (grad_hidden * activated).astype(jnp.bfloat16)
    grad_pregate = (
        grad_hidden * pre_up * sigmoid_gate * (1.0 + pre_gate * (1.0 - sigmoid_gate))
    ).astype(jnp.bfloat16)
    mix_partial = jnp.sum(hidden.astype(jnp.float32) * back_hidden, axis=1).astype(jnp.bfloat16)
    down_grad = lax.dot_general(
        hidden, scaled_cotan, contract_first, preferred_element_type=jnp.float32
    )
    gate_grad = lax.dot_general(
        row_tokens, grad_pregate, contract_first, preferred_element_type=jnp.float32
    )
    up_grad = lax.dot_general(
        row_tokens, grad_upper, contract_first, preferred_element_type=jnp.float32
    )
    joined_grad = jnp.concatenate([grad_pregate, grad_upper], axis=1)
    joined_weight = jnp.concatenate([gate_matrix, up_matrix], axis=1)
    token_partial = lax.dot_general(
        joined_grad, joined_weight, contract_last, preferred_element_type=jnp.float32
    ).astype(jnp.bfloat16)
    return (token_partial, mix_partial, gate_grad, up_grad, down_grad)


def local_exchange(tokens, cotangent, routes, mix_weights, gate_matrix, up_matrix, down_matrix):
    tok_count, features = tokens.shape
    top_count = routes.shape[1]
    columns = lax.axis_size("expert")
    dp_size = lax.axis_size("dp")
    team_size = dp_size // 2
    experts = 2 * columns
    slot_most = min(5 * tok_count * top_count // (4 * experts), tok_count)
    row_count = tok_count * top_count
    slot_count = experts * slot_most
    expert_ids = routes.reshape(row_count)
    onehot = (expert_ids[:, None] == jnp.arange(experts, dtype=jnp.int32)[None, :]).astype(
        jnp.bfloat16
    )
    row_index = jnp.arange(row_count, dtype=jnp.int32)
    earlier = (row_index[None, :] < row_index[:, None]).astype(jnp.bfloat16)
    prior_count = jnp.dot(earlier, onehot, preferred_element_type=jnp.float32)
    position = jnp.sum(prior_count * onehot.astype(jnp.float32), axis=1).astype(jnp.int32)
    slot_ids = expert_ids * slot_most + position
    slot_pick = (slot_ids[:, None] == jnp.arange(slot_count, dtype=jnp.int32)[None, :]).astype(
        jnp.bfloat16
    )
    token_rows = jnp.repeat(tokens, top_count, axis=0)
    cotan_rows = jnp.repeat(cotangent, top_count, axis=0)
    mix_rows = mix_weights.reshape(row_count, 1)
    pick_form = "rs,rd->sd"
    token_slots = jnp.einsum(
        pick_form, slot_pick, token_rows, preferred_element_type=jnp.float32
    ).astype(jnp.bfloat16)
    cotan_slots = jnp.einsum(
        pick_form, slot_pick, cotan_rows, preferred_element_type=jnp.float32
    ).astype(jnp.bfloat16)
    mix_slots = (
        jnp.einsum(pick_form, slot_pick, mix_rows, preferred_element_type=jnp.float32)
        .astype(jnp.bfloat16)
        .reshape(slot_count)
    )

    def spread(values):
        rest = values.shape[1:]
        lead = values.reshape((columns, 2, 1, slot_most) + rest)
        wide = jnp.broadcast_to(lead, (columns, 2, team_size, slot_most) + rest)
        return wide.reshape((columns, dp_size, slot_most) + rest)

    arrived = (
        lax.all_to_all(
            lax.all_to_all(spread(token_slots), "expert", split_axis=0, concat_axis=0, tiled=True),
            "dp",
            split_axis=1,
            concat_axis=1,
            tiled=True,
        ),
        lax.all_to_all(
            lax.all_to_all(spread(cotan_slots), "expert", split_axis=0, concat_axis=0, tiled=True),
            "dp",
            split_axis=1,
            concat_axis=1,
            tiled=True,
        ),
        lax.all_to_all(
            lax.all_to_all(spread(mix_slots), "expert", split_axis=0, concat_axis=0, tiled=True),
            "dp",
            split_axis=1,
            concat_axis=1,
            tiled=True,
        ),
    )
    token_partial, mix_partial, gate_grad, up_grad, down_grad = expert_backward(
        arrived[0].reshape(-1, features),
        arrived[1].reshape(-1, features),
        arrived[2].reshape(-1),
        gate_matrix,
        up_matrix,
        down_matrix,
    )
    returned = (
        lax.all_to_all(
            lax.all_to_all(
                token_partial.reshape(columns, dp_size, slot_most, features),
                "expert",
                split_axis=0,
                concat_axis=0,
                tiled=True,
            ),
            "dp",
            split_axis=1,
            concat_axis=1,
            tiled=True,
        ),
        lax.all_to_all(
            lax.all_to_all(
                mix_partial.reshape(columns, dp_size, slot_most),
                "expert",
                split_axis=0,
                concat_axis=0,
                tiled=True,
            ),
            "dp",
            split_axis=1,
            concat_axis=1,
            tiled=True,
        ),
    )
    token_sums = (
        returned[0]
        .reshape(columns, 2, team_size, slot_most, features)
        .astype(jnp.float32)
        .sum(axis=2)
        .reshape(slot_count, features)
    )
    mix_sums = (
        returned[1]
        .reshape(columns, 2, team_size, slot_most)
        .astype(jnp.float32)
        .sum(axis=2)
        .reshape(slot_count)
    )
    token_pick = slot_pick.reshape(tok_count, top_count, slot_count).astype(jnp.float32).sum(axis=1)
    grad_tokens = jnp.dot(token_pick, token_sums, precision=lax.Precision.HIGHEST).astype(
        jnp.bfloat16
    )
    grad_mix = jnp.dot(
        slot_pick.astype(jnp.float32), mix_sums[:, None], precision=lax.Precision.HIGHEST
    ).reshape(tok_count, top_count)
    return (grad_tokens, grad_mix, gate_grad, up_grad, down_grad)


def position():
    expert = lax.axis_index("expert")
    return lax.div(expert, 2), lax.rem(expert, 2), lax.axis_index("dp")


def device(z, core, x):
    return {"expert": z * 2 + core, "dp": x}


def greet(height, z, core, x):
    barrier = pltpu.get_barrier_semaphore()
    above, below = z < height - 1, z > 0

    def signal(target):
        pl.semaphore_signal(barrier, inc=1, device_id=target, device_id_type=pl.DeviceIdType.MESH)

    signal(device(z, 1 - core, x))
    signal(device(z, core, 1 - x))

    @pl.when(above)
    def _():
        signal(device(z + 1, core, x))

    @pl.when(below)
    def _():
        signal(device(z - 1, core, x))

    pl.semaphore_wait(barrier, 2 + above.astype(jnp.int32) + below.astype(jnp.int32))


def gather_kernel(height, own_ref, world_ref, send_sem, recv_sem, own_sem):
    z, core, x = position()
    greet(height, z, core, x)
    mine = (z * 2 + core) * 2 + x
    keep = pltpu.make_async_copy(own_ref, world_ref.at[mine], own_sem)
    keep.start()
    near = [0]
    for step in range(1, height):
        near += [-step, step]

    def each(act):
        for shift in near:
            for other in (0, 1):
                from_z = z + shift
                from_x = x if other == 0 else 1 - x

                @pl.when((from_z >= 0) & (from_z < height))
                def _():
                    slot = (from_z * 2 + core) * 2 + from_x
                    local = shift == 0 and other == 0
                    source = own_ref if local else world_ref.at[slot]

                    def copy(kind, target):
                        return pltpu.make_async_remote_copy(
                            src_ref=source,
                            dst_ref=world_ref.at[slot],
                            send_sem=send_sem.at[kind, slot],
                            recv_sem=recv_sem.at[slot],
                            device_id=target,
                            device_id_type=pl.DeviceIdType.MESH,
                        )

                    along = (core == 0) | (other == 0)
                    act(local, slot, [
                        (along & (z < height - 1) if shift <= 0 else None,
                         lambda: copy(0, device(z + 1, core, x))),
                        (along & (z > 0) if shift >= 0 else None,
                         lambda: copy(1, device(z - 1, core, x))),
                        ((core == 1) | (shift == 0) if other == 0 else None,
                         lambda: copy(2, device(z, core, 1 - x))),
                        (True, lambda: copy(3, device(z, 1 - core, x))),
                    ])

    def arrive(slot):
        pltpu.make_async_remote_copy(
            src_ref=world_ref.at[slot],
            dst_ref=world_ref.at[slot],
            send_sem=send_sem.at[0, slot],
            recv_sem=recv_sem.at[slot],
            device_id=device(z, 1 - core, x),
            device_id_type=pl.DeviceIdType.MESH,
        ).wait_recv()

    def forward(local, slot, moves):
        if not local:
            arrive(slot)
        for when, make in moves:
            if when is None:
                continue
            if when is True:
                make().start()
            else:
                @pl.when(when)
                def _():
                    make().start()

    def settle(local, slot, moves):
        for when, make in moves:
            if when is None:
                continue
            if when is True:
                make().wait_send()
            else:
                @pl.when(when)
                def _():
                    make().wait_send()

    each(forward)
    for from_z in range(height):
        for from_x in range(2):
            arrive((from_z * 2 + 1 - core) * 2 + from_x)
    each(settle)
    keep.wait()


def gather(own, height):
    slots = 4 * height
    vmem = pl.BlockSpec(memory_space=pltpu.VMEM)
    return pl.pallas_call(
        lambda *refs: gather_kernel(height, *refs),
        out_shape=jax.ShapeDtypeStruct((slots,) + own.shape, own.dtype),
        in_specs=[vmem],
        out_specs=vmem,
        scratch_shapes=[
            pltpu.SemaphoreType.DMA((4, slots)),
            pltpu.SemaphoreType.DMA((slots,)),
            pltpu.SemaphoreType.DMA,
        ],
        compiler_params=pltpu.CompilerParams(
            collective_id=0, has_side_effects=True, vmem_limit_bytes=24 * 1024 * 1024
        ),
    )(own)


def reduce_kernel(height, own_ref, out_ref, core_in, up_in, down_in, x_in, staged, total,
                  core_send, core_recv, flow_send, up_recv, down_recv, x_recv):
    z, core, x = position()
    greet(height, z, core, x)
    f32 = jnp.float32

    def move(source, target_ref, send, recv, target):
        return pltpu.make_async_remote_copy(
            src_ref=source, dst_ref=target_ref, send_sem=send, recv_sem=recv,
            device_id=target, device_id_type=pl.DeviceIdType.MESH,
        )

    far = []
    for step in range(height - 1, 0, -1):
        far += [step, -step]
    far += [0]

    def each(act):
        for shift in far:
            for other in (1, 0):
                to_z = z + shift
                to_x = x if other == 0 else 1 - x

                @pl.when((to_z >= 0) & (to_z < height))
                def _():
                    act(shift, other, to_z, to_x, to_z * 2 + to_x)

    def over_core(to_z, to_x, block):
        return move(
            own_ref.at[(to_z * 2 + 1 - core) * 2 + to_x], core_in.at[block],
            core_send.at[block], core_recv.at[block], device(z, 1 - core, x),
        )

    def over_x(to_z, block):
        return move(
            staged.at[block], x_in.at[to_z], flow_send.at[block], x_recv.at[to_z],
            device(z, core, 1 - x),
        )

    def over_up(block):
        return move(
            staged.at[block], up_in.at[block], flow_send.at[block], up_recv.at[block],
            device(z + 1, core, x),
        )

    def over_down(block):
        return move(
            staged.at[block], down_in.at[block], flow_send.at[block], down_recv.at[block],
            device(z - 1, core, x),
        )

    def add(ref):
        total[...] += ref[...].astype(f32)

    def launch(shift, other, to_z, to_x, block):
        over_core(to_z, to_x, block).start()

    def work(shift, other, to_z, to_x, block):
        over_core(to_z, to_x, block).wait_recv()
        total[...] = own_ref[(to_z * 2 + core) * 2 + to_x].astype(f32) + core_in[block].astype(f32)
        along = True if other == 0 else core == 0
        if other == 0:
            @pl.when((core == 1) | (shift == 0))
            def _():
                over_x(to_z, block).wait_recv()
                add(x_in.at[to_z])
        if shift >= 0:
            @pl.when(along & (z > 0))
            def _():
                over_up(block).wait_recv()
                add(up_in.at[block])
        if shift <= 0:
            @pl.when(along & (z < height - 1))
            def _():
                over_down(block).wait_recv()
                add(down_in.at[block])
        if shift == 0 and other == 0:
            out_ref[...] = total[...].astype(out_ref.dtype)
        else:
            staged[block] = total[...].astype(staged.dtype)
            flow(shift, other, to_z, block, lambda copy: copy.start())

    def flow(shift, other, to_z, block, act):
        if other == 1 and shift == 0:
            act(over_x(to_z, block))
            return
        passing = over_up if shift > 0 else over_down
        if other == 0:
            act(passing(block))
            return

        @pl.when(core == 0)
        def _():
            act(passing(block))

        @pl.when(core == 1)
        def _():
            act(over_x(to_z, block))

    def settle(shift, other, to_z, to_x, block):
        over_core(to_z, to_x, block).wait_send()
        if not (shift == 0 and other == 0):
            flow(shift, other, to_z, block, lambda copy: copy.wait_send())

    each(launch)
    each(work)
    each(settle)


def scatter_sum(parts, height):
    vmem = pl.BlockSpec(memory_space=pltpu.VMEM)
    block = parts.shape[1:]
    dma = pltpu.SemaphoreType.DMA
    half = 2 * height
    return pl.pallas_call(
        lambda *refs: reduce_kernel(height, *refs),
        out_shape=jax.ShapeDtypeStruct(block, parts.dtype),
        in_specs=[vmem],
        out_specs=vmem,
        scratch_shapes=[
            pltpu.VMEM((half,) + block, parts.dtype),
            pltpu.VMEM((half,) + block, parts.dtype),
            pltpu.VMEM((half,) + block, parts.dtype),
            pltpu.VMEM((height,) + block, parts.dtype),
            pltpu.VMEM((half,) + block, parts.dtype),
            pltpu.VMEM(block, jnp.float32),
            dma((half,)), dma((half,)), dma((half,)), dma((half,)), dma((half,)), dma((height,)),
        ],
        compiler_params=pltpu.CompilerParams(
            collective_id=1, has_side_effects=True, vmem_limit_bytes=24 * 1024 * 1024
        ),
    )(parts)


def local_gather(tokens, cotangent, routes, mix_weights, gate_matrix, up_matrix, down_matrix):
    f32, bf16 = jnp.float32, jnp.bfloat16
    tok_count, features = tokens.shape
    top_count = routes.shape[1]
    height = lax.axis_size("expert") // 2
    devices = experts = lax.axis_size("expert") * lax.axis_size("dp")
    slot_most = min(5 * tok_count * top_count // (4 * experts), tok_count)
    rows = devices * slot_most
    mine = lax.axis_index("expert") * lax.axis_size("dp") + lax.axis_index("dp")
    named = jnp.concatenate([routes.astype(bf16), mix_weights], axis=1)
    named = jnp.pad(named, ((0, tok_count), (0, 128 - 2 * top_count)))
    packed = jnp.concatenate(
        [jnp.concatenate([tokens, cotangent], axis=0), named], axis=1
    )
    world = gather(packed, height)
    named = world[:, :tok_count, features : features + top_count] == mine.astype(bf16)
    heavy = world[:, :tok_count, features + top_count : features + 2 * top_count]
    weight = jnp.sum(jnp.where(named, heavy, 0).astype(f32), axis=2)
    hit = jnp.any(named, axis=2)
    ahead = (
        jnp.arange(tok_count)[:, None] < jnp.arange(tok_count)[None, :]
    ).astype(bf16)
    place = jnp.dot(hit.astype(bf16), ahead, preferred_element_type=f32).astype(jnp.int32)
    place = place + jnp.arange(devices, dtype=jnp.int32)[:, None] * slot_most
    place = jnp.where(hit, place, -1)
    place_both = jnp.concatenate([place, jnp.where(hit, place + rows, -1)], axis=1)
    place_both = place_both.reshape(devices * 2 * tok_count)
    pick = (jnp.arange(2 * rows, dtype=jnp.int32)[:, None] == place_both[None, :]).astype(bf16)
    flat = world.reshape(devices * 2 * tok_count, world.shape[2])[:, :features]
    row_both = jnp.dot(pick, flat, preferred_element_type=f32).astype(bf16)
    weight_both = jnp.pad(weight, ((0, 0), (0, tok_count))).reshape(-1)
    row_mix = jnp.sum(pick[:rows].astype(f32) * weight_both[None, :], axis=1).astype(bf16)
    token_partial, mix_partial, gate_grad, up_grad, down_grad = expert_backward(
        row_both[:rows], row_both[rows:], row_mix, gate_matrix, up_matrix, down_matrix
    )
    lane = (jnp.arange(128, dtype=jnp.int32)[None, :] == mine).astype(bf16)
    half = features // 2
    back = jnp.concatenate(
        [
            jnp.concatenate([token_partial[:, :half], token_partial[:, half:]], axis=0),
            jnp.pad(mix_partial[:, None] * lane, ((0, rows), (0, 0))),
        ],
        axis=1,
    )
    spread = lax.dot_general(
        pick, back, (((0,), (0,)), ((), ())), preferred_element_type=f32
    ).astype(bf16)
    home = scatter_sum(spread.reshape(devices, 2 * tok_count, half + 128), height)
    grad_tokens = jnp.concatenate([home[:tok_count, :half], home[tok_count:, :half]], axis=1)
    chosen = routes[:, :, None] == jnp.arange(experts, dtype=jnp.int32)[None, None, :]
    grad_mix = jnp.sum(
        jnp.where(chosen, home[:tok_count, None, half : half + experts].astype(f32), 0.0), axis=2
    )
    return (grad_tokens, grad_mix, gate_grad, up_grad, down_grad)


def solution(mesh):
    local = local_gather if mesh.shape["dp"] == 2 else local_exchange
    in_specs = (
        P(("groups", "expert", "dp"), None),
        P(("groups", "expert", "dp"), None),
        P(("groups", "expert", "dp"), None),
        P(("groups", "expert", "dp"), None),
        P(None, ("expert", "dp")),
        P(None, ("expert", "dp")),
        P(("expert", "dp"), None),
    )
    out_specs = (
        P(("groups", "expert", "dp"), None),
        P(("groups", "expert", "dp"), None),
        P(None, ("groups", "expert", "dp")),
        P(None, ("groups", "expert", "dp")),
        P(("groups", "expert", "dp"), None),
    )
    return jax.shard_map(local, mesh=mesh, in_specs=in_specs, out_specs=out_specs, check_vma=False)
```

```python
import jax
import jax.numpy as jnp
from jax import lax
from jax.experimental import pallas as pl
from jax.experimental.pallas import tpu as pltpu
from jax.sharding import PartitionSpec as P


def expert_backward(row_tokens, row_cotan, row_mix, gate_matrix, up_matrix, down_matrix):
    contract_last = (((1,), (1,)), ((), ()))
    contract_first = (((0,), (0,)), ((), ()))
    pre_gate = jnp.dot(row_tokens, gate_matrix, preferred_element_type=jnp.float32)
    pre_up = jnp.dot(row_tokens, up_matrix, preferred_element_type=jnp.float32)
    sigmoid_gate = jax.nn.sigmoid(pre_gate)
    activated = pre_gate * sigmoid_gate
    hidden = (activated * pre_up).astype(jnp.bfloat16)
    back_hidden = lax.dot_general(
        row_cotan, down_matrix, contract_last, preferred_element_type=jnp.float32
    )
    mix_column = row_mix.astype(jnp.float32)[:, None]
    scaled_cotan = (mix_column * row_cotan.astype(jnp.float32)).astype(jnp.bfloat16)
    grad_hidden = mix_column * back_hidden
    grad_upper = (grad_hidden * activated).astype(jnp.bfloat16)
    grad_pregate = (
        grad_hidden * pre_up * sigmoid_gate * (1.0 + pre_gate * (1.0 - sigmoid_gate))
    ).astype(jnp.bfloat16)
    mix_partial = jnp.sum(hidden.astype(jnp.float32) * back_hidden, axis=1).astype(jnp.bfloat16)
    down_grad = lax.dot_general(
        hidden, scaled_cotan, contract_first, preferred_element_type=jnp.float32
    )
    gate_grad = lax.dot_general(
        row_tokens, grad_pregate, contract_first, preferred_element_type=jnp.float32
    )
    up_grad = lax.dot_general(
        row_tokens, grad_upper, contract_first, preferred_element_type=jnp.float32
    )
    joined_grad = jnp.concatenate([grad_pregate, grad_upper], axis=1)
    joined_weight = jnp.concatenate([gate_matrix, up_matrix], axis=1)
    token_partial = lax.dot_general(
        joined_grad, joined_weight, contract_last, preferred_element_type=jnp.float32
    ).astype(jnp.bfloat16)
    return (token_partial, mix_partial, gate_grad, up_grad, down_grad)


def local_exchange(tokens, cotangent, routes, mix_weights, gate_matrix, up_matrix, down_matrix):
    tok_count, features = tokens.shape
    top_count = routes.shape[1]
    columns = lax.axis_size("expert")
    dp_size = lax.axis_size("dp")
    team_size = dp_size // 2
    experts = 2 * columns
    slot_most = min(5 * tok_count * top_count // (4 * experts), tok_count)
    row_count = tok_count * top_count
    slot_count = experts * slot_most
    expert_ids = routes.reshape(row_count)
    onehot = (expert_ids[:, None] == jnp.arange(experts, dtype=jnp.int32)[None, :]).astype(
        jnp.bfloat16
    )
    row_index = jnp.arange(row_count, dtype=jnp.int32)
    earlier = (row_index[None, :] < row_index[:, None]).astype(jnp.bfloat16)
    prior_count = jnp.dot(earlier, onehot, preferred_element_type=jnp.float32)
    position = jnp.sum(prior_count * onehot.astype(jnp.float32), axis=1).astype(jnp.int32)
    slot_ids = expert_ids * slot_most + position
    slot_pick = (slot_ids[:, None] == jnp.arange(slot_count, dtype=jnp.int32)[None, :]).astype(
        jnp.bfloat16
    )
    token_rows = jnp.repeat(tokens, top_count, axis=0)
    cotan_rows = jnp.repeat(cotangent, top_count, axis=0)
    mix_rows = mix_weights.reshape(row_count, 1)
    pick_form = "rs,rd->sd"
    token_slots = jnp.einsum(
        pick_form, slot_pick, token_rows, preferred_element_type=jnp.float32
    ).astype(jnp.bfloat16)
    cotan_slots = jnp.einsum(
        pick_form, slot_pick, cotan_rows, preferred_element_type=jnp.float32
    ).astype(jnp.bfloat16)
    mix_slots = (
        jnp.einsum(pick_form, slot_pick, mix_rows, preferred_element_type=jnp.float32)
        .astype(jnp.bfloat16)
        .reshape(slot_count)
    )

    def spread(values):
        rest = values.shape[1:]
        lead = values.reshape((columns, 2, 1, slot_most) + rest)
        wide = jnp.broadcast_to(lead, (columns, 2, team_size, slot_most) + rest)
        return wide.reshape((columns, dp_size, slot_most) + rest)

    arrived = (
        lax.all_to_all(
            lax.all_to_all(spread(token_slots), "expert", split_axis=0, concat_axis=0, tiled=True),
            "dp",
            split_axis=1,
            concat_axis=1,
            tiled=True,
        ),
        lax.all_to_all(
            lax.all_to_all(spread(cotan_slots), "expert", split_axis=0, concat_axis=0, tiled=True),
            "dp",
            split_axis=1,
            concat_axis=1,
            tiled=True,
        ),
        lax.all_to_all(
            lax.all_to_all(spread(mix_slots), "expert", split_axis=0, concat_axis=0, tiled=True),
            "dp",
            split_axis=1,
            concat_axis=1,
            tiled=True,
        ),
    )
    token_partial, mix_partial, gate_grad, up_grad, down_grad = expert_backward(
        arrived[0].reshape(-1, features),
        arrived[1].reshape(-1, features),
        arrived[2].reshape(-1),
        gate_matrix,
        up_matrix,
        down_matrix,
    )
    returned = (
        lax.all_to_all(
            lax.all_to_all(
                token_partial.reshape(columns, dp_size, slot_most, features),
                "expert",
                split_axis=0,
                concat_axis=0,
                tiled=True,
            ),
            "dp",
            split_axis=1,
            concat_axis=1,
            tiled=True,
        ),
        lax.all_to_all(
            lax.all_to_all(
                mix_partial.reshape(columns, dp_size, slot_most),
                "expert",
                split_axis=0,
                concat_axis=0,
                tiled=True,
            ),
            "dp",
            split_axis=1,
            concat_axis=1,
            tiled=True,
        ),
    )
    token_sums = (
        returned[0]
        .reshape(columns, 2, team_size, slot_most, features)
        .astype(jnp.float32)
        .sum(axis=2)
        .reshape(slot_count, features)
    )
    mix_sums = (
        returned[1]
        .reshape(columns, 2, team_size, slot_most)
        .astype(jnp.float32)
        .sum(axis=2)
        .reshape(slot_count)
    )
    token_pick = slot_pick.reshape(tok_count, top_count, slot_count).astype(jnp.float32).sum(axis=1)
    grad_tokens = jnp.dot(token_pick, token_sums, precision=lax.Precision.HIGHEST).astype(
        jnp.bfloat16
    )
    grad_mix = jnp.dot(
        slot_pick.astype(jnp.float32), mix_sums[:, None], precision=lax.Precision.HIGHEST
    ).reshape(tok_count, top_count)
    return (grad_tokens, grad_mix, gate_grad, up_grad, down_grad)


def position():
    expert = lax.axis_index("expert")
    return lax.div(expert, 2), lax.rem(expert, 2), lax.axis_index("dp")


def device(z, core, x):
    return {"expert": z * 2 + core, "dp": x}


def greet(height, z, core, x):
    barrier = pltpu.get_barrier_semaphore()
    above, below = z < height - 1, z > 0

    def signal(target):
        pl.semaphore_signal(barrier, inc=1, device_id=target, device_id_type=pl.DeviceIdType.MESH)

    signal(device(z, 1 - core, x))
    signal(device(z, core, 1 - x))

    @pl.when(above)
    def _():
        signal(device(z + 1, core, x))

    @pl.when(below)
    def _():
        signal(device(z - 1, core, x))

    pl.semaphore_wait(barrier, 2 + above.astype(jnp.int32) + below.astype(jnp.int32))


def gather_kernel(height, own_ref, world_ref, send_sem, recv_sem, own_sem):
    z, core, x = position()
    greet(height, z, core, x)
    mine = (z * 2 + core) * 2 + x
    keep = pltpu.make_async_copy(own_ref, world_ref.at[mine], own_sem)
    keep.start()
    near = [0]
    for step in range(1, height):
        near += [-step, step]

    cut = own_ref.shape[0] // 48 * 32
    pieces = (pl.ds(0, cut), pl.ds(cut, own_ref.shape[0] - cut))

    def each(act):
        for shift in near:
            for other, piece in ((0, 0), (0, 1), (1, 0), (1, 1)):
                from_z = z + shift
                from_x = x if other == 0 else 1 - x

                @pl.when((from_z >= 0) & (from_z < height))
                def _():
                    slot = (from_z * 2 + core) * 2 + from_x
                    local = shift == 0 and other == 0
                    part = world_ref.at[slot, pieces[piece]]
                    source = own_ref.at[pieces[piece]] if local else part

                    def copy(kind, target):
                        return pltpu.make_async_remote_copy(
                            src_ref=source,
                            dst_ref=part,
                            send_sem=send_sem.at[kind, slot, piece],
                            recv_sem=recv_sem.at[slot, piece],
                            device_id=target,
                            device_id_type=pl.DeviceIdType.MESH,
                        )

                    along = (core == 0) | (other == 0)
                    act(local, slot, piece, [
                        (along & (z < height - 1) if shift <= 0 else None,
                         lambda: copy(0, device(z + 1, core, x))),
                        (along & (z > 0) if shift >= 0 else None,
                         lambda: copy(1, device(z - 1, core, x))),
                        ((core == 1) | (shift == 0) if other == 0 else None,
                         lambda: copy(2, device(z, core, 1 - x))),
                        (True, lambda: copy(3, device(z, 1 - core, x))),
                    ])

    def arrive(slot, piece):
        pltpu.make_async_remote_copy(
            src_ref=world_ref.at[slot, pieces[piece]],
            dst_ref=world_ref.at[slot, pieces[piece]],
            send_sem=send_sem.at[0, slot, piece],
            recv_sem=recv_sem.at[slot, piece],
            device_id=device(z, 1 - core, x),
            device_id_type=pl.DeviceIdType.MESH,
        ).wait_recv()

    def forward(local, slot, piece, moves):
        if not local:
            arrive(slot, piece)
        for when, make in moves:
            if when is None:
                continue
            if when is True:
                make().start()
            else:
                @pl.when(when)
                def _():
                    make().start()

    def settle(local, slot, piece, moves):
        for when, make in moves:
            if when is None:
                continue
            if when is True:
                make().wait_send()
            else:
                @pl.when(when)
                def _():
                    make().wait_send()

    each(forward)
    for from_z in range(height):
        for from_x in range(2):
            for piece in range(2):
                arrive((from_z * 2 + 1 - core) * 2 + from_x, piece)
    each(settle)
    keep.wait()


def gather(own, height):
    slots = 4 * height
    vmem = pl.BlockSpec(memory_space=pltpu.VMEM)
    return pl.pallas_call(
        lambda *refs: gather_kernel(height, *refs),
        out_shape=jax.ShapeDtypeStruct((slots,) + own.shape, own.dtype),
        in_specs=[vmem],
        out_specs=vmem,
        scratch_shapes=[
            pltpu.SemaphoreType.DMA((4, slots, 2)),
            pltpu.SemaphoreType.DMA((slots, 2)),
            pltpu.SemaphoreType.DMA,
        ],
        compiler_params=pltpu.CompilerParams(
            collective_id=0, has_side_effects=True, vmem_limit_bytes=24 * 1024 * 1024
        ),
    )(own)


def reduce_kernel(height, own_ref, out_ref, core_in, up_in, down_in, x_in, staged, total,
                  core_send, core_recv, flow_send, up_recv, down_recv, x_recv):
    z, core, x = position()
    greet(height, z, core, x)
    f32 = jnp.float32

    def move(source, target_ref, send, recv, target):
        return pltpu.make_async_remote_copy(
            src_ref=source, dst_ref=target_ref, send_sem=send, recv_sem=recv,
            device_id=target, device_id_type=pl.DeviceIdType.MESH,
        )

    far = []
    for step in range(height - 1, 0, -1):
        far += [step, -step]
    far += [0]

    def each(act):
        for shift in far:
            for other in (1, 0):
                to_z = z + shift
                to_x = x if other == 0 else 1 - x

                @pl.when((to_z >= 0) & (to_z < height))
                def _():
                    act(shift, other, to_z, to_x, to_z * 2 + to_x)

    def over_core(to_z, to_x, block):
        return move(
            own_ref.at[(to_z * 2 + 1 - core) * 2 + to_x], core_in.at[block],
            core_send.at[block], core_recv.at[block], device(z, 1 - core, x),
        )

    def over_x(to_z, block):
        return move(
            staged.at[block], x_in.at[to_z], flow_send.at[block], x_recv.at[to_z],
            device(z, core, 1 - x),
        )

    def over_up(block):
        return move(
            staged.at[block], up_in.at[block], flow_send.at[block], up_recv.at[block],
            device(z + 1, core, x),
        )

    def over_down(block):
        return move(
            staged.at[block], down_in.at[block], flow_send.at[block], down_recv.at[block],
            device(z - 1, core, x),
        )

    def add(ref):
        total[...] += ref[...].astype(f32)

    def launch(shift, other, to_z, to_x, block):
        over_core(to_z, to_x, block).start()

    def work(shift, other, to_z, to_x, block):
        over_core(to_z, to_x, block).wait_recv()
        total[...] = own_ref[(to_z * 2 + core) * 2 + to_x].astype(f32) + core_in[block].astype(f32)
        along = True if other == 0 else core == 0
        if other == 0:
            @pl.when((core == 1) | (shift == 0))
            def _():
                over_x(to_z, block).wait_recv()
                add(x_in.at[to_z])
        if shift >= 0:
            @pl.when(along & (z > 0))
            def _():
                over_up(block).wait_recv()
                add(up_in.at[block])
        if shift <= 0:
            @pl.when(along & (z < height - 1))
            def _():
                over_down(block).wait_recv()
                add(down_in.at[block])
        if shift == 0 and other == 0:
            out_ref[...] = total[...].astype(out_ref.dtype)
        else:
            staged[block] = total[...].astype(staged.dtype)
            flow(shift, other, to_z, block, lambda copy: copy.start())

    def flow(shift, other, to_z, block, act):
        if other == 1 and shift == 0:
            act(over_x(to_z, block))
            return
        passing = over_up if shift > 0 else over_down
        if other == 0:
            act(passing(block))
            return

        @pl.when(core == 0)
        def _():
            act(passing(block))

        @pl.when(core == 1)
        def _():
            act(over_x(to_z, block))

    def settle(shift, other, to_z, to_x, block):
        over_core(to_z, to_x, block).wait_send()
        if not (shift == 0 and other == 0):
            flow(shift, other, to_z, block, lambda copy: copy.wait_send())

    each(launch)
    each(work)
    each(settle)


def scatter_sum(parts, height):
    vmem = pl.BlockSpec(memory_space=pltpu.VMEM)
    block = parts.shape[1:]
    dma = pltpu.SemaphoreType.DMA
    half = 2 * height
    return pl.pallas_call(
        lambda *refs: reduce_kernel(height, *refs),
        out_shape=jax.ShapeDtypeStruct(block, parts.dtype),
        in_specs=[vmem],
        out_specs=vmem,
        scratch_shapes=[
            pltpu.VMEM((half,) + block, parts.dtype),
            pltpu.VMEM((half,) + block, parts.dtype),
            pltpu.VMEM((half,) + block, parts.dtype),
            pltpu.VMEM((height,) + block, parts.dtype),
            pltpu.VMEM((half,) + block, parts.dtype),
            pltpu.VMEM(block, jnp.float32),
            dma((half,)), dma((half,)), dma((half,)), dma((half,)), dma((half,)), dma((height,)),
        ],
        compiler_params=pltpu.CompilerParams(
            collective_id=1, has_side_effects=True, vmem_limit_bytes=24 * 1024 * 1024
        ),
    )(parts)


def local_gather(tokens, cotangent, routes, mix_weights, gate_matrix, up_matrix, down_matrix):
    f32, bf16 = jnp.float32, jnp.bfloat16
    tok_count, features = tokens.shape
    top_count = routes.shape[1]
    height = lax.axis_size("expert") // 2
    devices = experts = lax.axis_size("expert") * lax.axis_size("dp")
    slot_most = min(5 * tok_count * top_count // (4 * experts), tok_count)
    rows = devices * slot_most
    mine = lax.axis_index("expert") * lax.axis_size("dp") + lax.axis_index("dp")
    named = jnp.concatenate([routes.astype(bf16), mix_weights], axis=1)
    named = jnp.pad(named, ((0, tok_count), (0, 128 - 2 * top_count)))
    packed = jnp.concatenate(
        [jnp.concatenate([tokens, cotangent], axis=0), named], axis=1
    )
    world = gather(packed, height)
    named = world[:, :tok_count, features : features + top_count] == mine.astype(bf16)
    heavy = world[:, :tok_count, features + top_count : features + 2 * top_count]
    weight = jnp.sum(jnp.where(named, heavy, 0).astype(f32), axis=2)
    hit = jnp.any(named, axis=2)
    ahead = (
        jnp.arange(tok_count)[:, None] < jnp.arange(tok_count)[None, :]
    ).astype(bf16)
    place = jnp.dot(hit.astype(bf16), ahead, preferred_element_type=f32).astype(jnp.int32)
    place = place + jnp.arange(devices, dtype=jnp.int32)[:, None] * slot_most
    place = jnp.where(hit, place, -1)
    place_both = jnp.concatenate([place, jnp.where(hit, place + rows, -1)], axis=1)
    place_both = place_both.reshape(devices * 2 * tok_count)
    pick = (jnp.arange(2 * rows, dtype=jnp.int32)[:, None] == place_both[None, :]).astype(bf16)
    flat = world.reshape(devices * 2 * tok_count, world.shape[2])[:, :features]
    row_both = jnp.dot(pick, flat, preferred_element_type=f32).astype(bf16)
    weight_both = jnp.pad(weight, ((0, 0), (0, tok_count))).reshape(-1)
    row_mix = jnp.sum(pick[:rows].astype(f32) * weight_both[None, :], axis=1).astype(bf16)
    token_partial, mix_partial, gate_grad, up_grad, down_grad = expert_backward(
        row_both[:rows], row_both[rows:], row_mix, gate_matrix, up_matrix, down_matrix
    )
    lane = (jnp.arange(128, dtype=jnp.int32)[None, :] == mine).astype(bf16)
    half = features // 2
    back = jnp.concatenate(
        [
            jnp.concatenate([token_partial[:, :half], token_partial[:, half:]], axis=0),
            jnp.pad(mix_partial[:, None] * lane, ((0, rows), (0, 0))),
        ],
        axis=1,
    )
    spread = lax.dot_general(
        pick, back, (((0,), (0,)), ((), ())), preferred_element_type=f32
    ).astype(bf16)
    home = scatter_sum(spread.reshape(devices, 2 * tok_count, half + 128), height)
    grad_tokens = jnp.concatenate([home[:tok_count, :half], home[tok_count:, :half]], axis=1)
    chosen = routes[:, :, None] == jnp.arange(experts, dtype=jnp.int32)[None, None, :]
    grad_mix = jnp.sum(
        jnp.where(chosen, home[:tok_count, None, half : half + experts].astype(f32), 0.0), axis=2
    )
    return (grad_tokens, grad_mix, gate_grad, up_grad, down_grad)


def solution(mesh):
    local = local_gather if mesh.shape["dp"] == 2 else local_exchange
    in_specs = (
        P(("groups", "expert", "dp"), None),
        P(("groups", "expert", "dp"), None),
        P(("groups", "expert", "dp"), None),
        P(("groups", "expert", "dp"), None),
        P(None, ("expert", "dp")),
        P(None, ("expert", "dp")),
        P(("expert", "dp"), None),
    )
    out_specs = (
        P(("groups", "expert", "dp"), None),
        P(("groups", "expert", "dp"), None),
        P(None, ("groups", "expert", "dp")),
        P(None, ("groups", "expert", "dp")),
        P(("groups", "expert", "dp"), None),
    )
    return jax.shard_map(local, mesh=mesh, in_specs=in_specs, out_specs=out_specs, check_vma=False)
```

```python
import jax
import jax.numpy as jnp
from jax import lax
from jax.experimental import pallas as pl
from jax.experimental.pallas import tpu as pltpu
from jax.sharding import PartitionSpec as P


def weight_kernel(x_ref, gate_ref, up_ref, hidden_ref, cotan_ref, dgate_ref, dup_ref, ddown_ref):
    contract_first = (((0,), (0,)), ((), ()))
    for left, right, out in (
        (x_ref, gate_ref, dgate_ref),
        (x_ref, up_ref, dup_ref),
        (hidden_ref, cotan_ref, ddown_ref),
    ):
        out[...] = lax.dot_general(
            left[...], right[...], contract_first, preferred_element_type=jnp.float32
        )


def weight_grads(rows_x, rows_gate, rows_up, rows_hidden, rows_cotan):
    rows, features = rows_x.shape
    units = rows_hidden.shape[1]
    steps = 8
    whole = lambda width: pl.BlockSpec((rows, width), lambda i: (0, 0))
    piece = lambda width: pl.BlockSpec((rows, width // steps), lambda i: (0, i))
    result = lambda height, width: pl.BlockSpec((height // steps, width), lambda i: (i, 0))
    shape = lambda height, width: jax.ShapeDtypeStruct((height, width), jnp.float32)
    return pl.pallas_call(
        weight_kernel,
        grid=(steps,),
        in_specs=[piece(features), whole(units), whole(units), piece(units), whole(features)],
        out_specs=[result(features, units), result(features, units), result(units, features)],
        out_shape=[shape(features, units), shape(features, units), shape(units, features)],
        compiler_params=pltpu.CompilerParams(vmem_limit_bytes=32 * 1024 * 1024),
        cost_estimate=pl.CostEstimate(
            flops=6 * rows * features * units,
            bytes_accessed=12 * features * units,
            transcendentals=0,
        ),
    )(rows_x, rows_gate, rows_up, rows_hidden, rows_cotan)


def expert_backward(
    row_tokens, row_cotan, row_mix, gate_matrix, up_matrix, down_matrix, tiled=False
):
    contract_last = (((1,), (1,)), ((), ()))
    contract_first = (((0,), (0,)), ((), ()))
    pre_gate = jnp.dot(row_tokens, gate_matrix, preferred_element_type=jnp.float32)
    pre_up = jnp.dot(row_tokens, up_matrix, preferred_element_type=jnp.float32)
    sigmoid_gate = jax.nn.sigmoid(pre_gate)
    activated = pre_gate * sigmoid_gate
    hidden = (activated * pre_up).astype(jnp.bfloat16)
    back_hidden = lax.dot_general(
        row_cotan, down_matrix, contract_last, preferred_element_type=jnp.float32
    )
    mix_column = row_mix.astype(jnp.float32)[:, None]
    scaled_cotan = (mix_column * row_cotan.astype(jnp.float32)).astype(jnp.bfloat16)
    grad_hidden = mix_column * back_hidden
    grad_upper = (grad_hidden * activated).astype(jnp.bfloat16)
    grad_pregate = (
        grad_hidden * pre_up * sigmoid_gate * (1.0 + pre_gate * (1.0 - sigmoid_gate))
    ).astype(jnp.bfloat16)
    mix_partial = jnp.sum(hidden.astype(jnp.float32) * back_hidden, axis=1).astype(jnp.bfloat16)
    if tiled:
        gate_grad, up_grad, down_grad = weight_grads(
            row_tokens, grad_pregate, grad_upper, hidden, scaled_cotan
        )
    else:
        down_grad = lax.dot_general(
            hidden, scaled_cotan, contract_first, preferred_element_type=jnp.float32
        )
        gate_grad = lax.dot_general(
            row_tokens, grad_pregate, contract_first, preferred_element_type=jnp.float32
        )
        up_grad = lax.dot_general(
            row_tokens, grad_upper, contract_first, preferred_element_type=jnp.float32
        )
    joined_grad = jnp.concatenate([grad_pregate, grad_upper], axis=1)
    joined_weight = jnp.concatenate([gate_matrix, up_matrix], axis=1)
    token_partial = lax.dot_general(
        joined_grad, joined_weight, contract_last, preferred_element_type=jnp.float32
    ).astype(jnp.bfloat16)
    return (token_partial, mix_partial, gate_grad, up_grad, down_grad)


def local_exchange(tokens, cotangent, routes, mix_weights, gate_matrix, up_matrix, down_matrix):
    tok_count, features = tokens.shape
    top_count = routes.shape[1]
    columns = lax.axis_size("expert")
    dp_size = lax.axis_size("dp")
    team_size = dp_size // 2
    experts = 2 * columns
    slot_most = min(5 * tok_count * top_count // (4 * experts), tok_count)
    row_count = tok_count * top_count
    slot_count = experts * slot_most
    expert_ids = routes.reshape(row_count)
    onehot = (expert_ids[:, None] == jnp.arange(experts, dtype=jnp.int32)[None, :]).astype(
        jnp.bfloat16
    )
    row_index = jnp.arange(row_count, dtype=jnp.int32)
    earlier = (row_index[None, :] < row_index[:, None]).astype(jnp.bfloat16)
    prior_count = jnp.dot(earlier, onehot, preferred_element_type=jnp.float32)
    position = jnp.sum(prior_count * onehot.astype(jnp.float32), axis=1).astype(jnp.int32)
    slot_ids = expert_ids * slot_most + position
    slot_pick = (slot_ids[:, None] == jnp.arange(slot_count, dtype=jnp.int32)[None, :]).astype(
        jnp.bfloat16
    )
    token_rows = jnp.repeat(tokens, top_count, axis=0)
    cotan_rows = jnp.repeat(cotangent, top_count, axis=0)
    mix_rows = mix_weights.reshape(row_count, 1)
    pick_form = "rs,rd->sd"
    token_slots = jnp.einsum(
        pick_form, slot_pick, token_rows, preferred_element_type=jnp.float32
    ).astype(jnp.bfloat16)
    cotan_slots = jnp.einsum(
        pick_form, slot_pick, cotan_rows, preferred_element_type=jnp.float32
    ).astype(jnp.bfloat16)
    mix_slots = (
        jnp.einsum(pick_form, slot_pick, mix_rows, preferred_element_type=jnp.float32)
        .astype(jnp.bfloat16)
        .reshape(slot_count)
    )

    def spread(values):
        rest = values.shape[1:]
        lead = values.reshape((columns, 2, 1, slot_most) + rest)
        wide = jnp.broadcast_to(lead, (columns, 2, team_size, slot_most) + rest)
        return wide.reshape((columns, dp_size, slot_most) + rest)

    arrived = (
        lax.all_to_all(
            lax.all_to_all(spread(token_slots), "expert", split_axis=0, concat_axis=0, tiled=True),
            "dp",
            split_axis=1,
            concat_axis=1,
            tiled=True,
        ),
        lax.all_to_all(
            lax.all_to_all(spread(cotan_slots), "expert", split_axis=0, concat_axis=0, tiled=True),
            "dp",
            split_axis=1,
            concat_axis=1,
            tiled=True,
        ),
        lax.all_to_all(
            lax.all_to_all(spread(mix_slots), "expert", split_axis=0, concat_axis=0, tiled=True),
            "dp",
            split_axis=1,
            concat_axis=1,
            tiled=True,
        ),
    )
    token_partial, mix_partial, gate_grad, up_grad, down_grad = expert_backward(
        arrived[0].reshape(-1, features),
        arrived[1].reshape(-1, features),
        arrived[2].reshape(-1),
        gate_matrix,
        up_matrix,
        down_matrix,
    )
    returned = (
        lax.all_to_all(
            lax.all_to_all(
                token_partial.reshape(columns, dp_size, slot_most, features),
                "expert",
                split_axis=0,
                concat_axis=0,
                tiled=True,
            ),
            "dp",
            split_axis=1,
            concat_axis=1,
            tiled=True,
        ),
        lax.all_to_all(
            lax.all_to_all(
                mix_partial.reshape(columns, dp_size, slot_most),
                "expert",
                split_axis=0,
                concat_axis=0,
                tiled=True,
            ),
            "dp",
            split_axis=1,
            concat_axis=1,
            tiled=True,
        ),
    )
    token_sums = (
        returned[0]
        .reshape(columns, 2, team_size, slot_most, features)
        .astype(jnp.float32)
        .sum(axis=2)
        .reshape(slot_count, features)
    )
    mix_sums = (
        returned[1]
        .reshape(columns, 2, team_size, slot_most)
        .astype(jnp.float32)
        .sum(axis=2)
        .reshape(slot_count)
    )
    token_pick = slot_pick.reshape(tok_count, top_count, slot_count).astype(jnp.float32).sum(axis=1)
    grad_tokens = jnp.dot(token_pick, token_sums, precision=lax.Precision.HIGHEST).astype(
        jnp.bfloat16
    )
    grad_mix = jnp.dot(
        slot_pick.astype(jnp.float32), mix_sums[:, None], precision=lax.Precision.HIGHEST
    ).reshape(tok_count, top_count)
    return (grad_tokens, grad_mix, gate_grad, up_grad, down_grad)


def position():
    expert = lax.axis_index("expert")
    return lax.div(expert, 2), lax.rem(expert, 2), lax.axis_index("dp")


def device(z, core, x):
    return {"expert": z * 2 + core, "dp": x}


def greet(height, z, core, x):
    barrier = pltpu.get_barrier_semaphore()
    above, below = z < height - 1, z > 0

    def signal(target):
        pl.semaphore_signal(barrier, inc=1, device_id=target, device_id_type=pl.DeviceIdType.MESH)

    signal(device(z, 1 - core, x))
    signal(device(z, core, 1 - x))

    @pl.when(above)
    def _():
        signal(device(z + 1, core, x))

    @pl.when(below)
    def _():
        signal(device(z - 1, core, x))

    pl.semaphore_wait(barrier, 2 + above.astype(jnp.int32) + below.astype(jnp.int32))


def gather_kernel(height, own_ref, world_ref, send_sem, recv_sem, own_sem):
    z, core, x = position()
    greet(height, z, core, x)
    mine = (z * 2 + core) * 2 + x
    keep = pltpu.make_async_copy(own_ref, world_ref.at[mine], own_sem)
    keep.start()
    near = [0]
    for step in range(1, height):
        near += [-step, step]

    cut = own_ref.shape[0] // 48 * 32
    pieces = (pl.ds(0, cut), pl.ds(cut, own_ref.shape[0] - cut))

    def each(act):
        for shift in near:
            for other, piece in ((0, 0), (0, 1), (1, 0), (1, 1)):
                from_z = z + shift
                from_x = x if other == 0 else 1 - x

                @pl.when((from_z >= 0) & (from_z < height))
                def _():
                    slot = (from_z * 2 + core) * 2 + from_x
                    local = shift == 0 and other == 0
                    part = world_ref.at[slot, pieces[piece]]
                    source = own_ref.at[pieces[piece]] if local else part

                    def copy(kind, target):
                        return pltpu.make_async_remote_copy(
                            src_ref=source,
                            dst_ref=part,
                            send_sem=send_sem.at[kind, slot, piece],
                            recv_sem=recv_sem.at[slot, piece],
                            device_id=target,
                            device_id_type=pl.DeviceIdType.MESH,
                        )

                    along = (core == 0) | (other == 0)
                    act(local, slot, piece, [
                        (along & (z < height - 1) if shift <= 0 else None,
                         lambda: copy(0, device(z + 1, core, x))),
                        (along & (z > 0) if shift >= 0 else None,
                         lambda: copy(1, device(z - 1, core, x))),
                        ((core == 1) | (shift == 0) if other == 0 else None,
                         lambda: copy(2, device(z, core, 1 - x))),
                        (True, lambda: copy(3, device(z, 1 - core, x))),
                    ])

    def arrive(slot, piece):
        pltpu.make_async_remote_copy(
            src_ref=world_ref.at[slot, pieces[piece]],
            dst_ref=world_ref.at[slot, pieces[piece]],
            send_sem=send_sem.at[0, slot, piece],
            recv_sem=recv_sem.at[slot, piece],
            device_id=device(z, 1 - core, x),
            device_id_type=pl.DeviceIdType.MESH,
        ).wait_recv()

    def forward(local, slot, piece, moves):
        if not local:
            arrive(slot, piece)
        for when, make in moves:
            if when is None:
                continue
            if when is True:
                make().start()
            else:
                @pl.when(when)
                def _():
                    make().start()

    def settle(local, slot, piece, moves):
        for when, make in moves:
            if when is None:
                continue
            if when is True:
                make().wait_send()
            else:
                @pl.when(when)
                def _():
                    make().wait_send()

    each(forward)
    for from_z in range(height):
        for from_x in range(2):
            for piece in range(2):
                arrive((from_z * 2 + 1 - core) * 2 + from_x, piece)
    each(settle)
    keep.wait()


def gather(own, height):
    slots = 4 * height
    vmem = pl.BlockSpec(memory_space=pltpu.VMEM)
    return pl.pallas_call(
        lambda *refs: gather_kernel(height, *refs),
        out_shape=jax.ShapeDtypeStruct((slots,) + own.shape, own.dtype),
        in_specs=[vmem],
        out_specs=vmem,
        scratch_shapes=[
            pltpu.SemaphoreType.DMA((4, slots, 2)),
            pltpu.SemaphoreType.DMA((slots, 2)),
            pltpu.SemaphoreType.DMA,
        ],
        compiler_params=pltpu.CompilerParams(
            collective_id=0, has_side_effects=True, vmem_limit_bytes=24 * 1024 * 1024
        ),
    )(own)


def reduce_kernel(height, own_ref, out_ref, core_in, up_in, down_in, x_in, staged, total,
                  core_send, core_recv, flow_send, up_recv, down_recv, x_recv):
    z, core, x = position()
    greet(height, z, core, x)
    f32 = jnp.float32

    def move(source, target_ref, send, recv, target):
        return pltpu.make_async_remote_copy(
            src_ref=source, dst_ref=target_ref, send_sem=send, recv_sem=recv,
            device_id=target, device_id_type=pl.DeviceIdType.MESH,
        )

    far = []
    for step in range(height - 1, 0, -1):
        far += [step, -step]
    far += [0]

    def each(act):
        for shift in far:
            for other in (1, 0):
                to_z = z + shift
                to_x = x if other == 0 else 1 - x

                @pl.when((to_z >= 0) & (to_z < height))
                def _():
                    act(shift, other, to_z, to_x, to_z * 2 + to_x)

    def over_core(to_z, to_x, block):
        return move(
            own_ref.at[(to_z * 2 + 1 - core) * 2 + to_x], core_in.at[block],
            core_send.at[block], core_recv.at[block], device(z, 1 - core, x),
        )

    def over_x(to_z, block):
        return move(
            staged.at[block], x_in.at[to_z], flow_send.at[block], x_recv.at[to_z],
            device(z, core, 1 - x),
        )

    def over_up(block):
        return move(
            staged.at[block], up_in.at[block], flow_send.at[block], up_recv.at[block],
            device(z + 1, core, x),
        )

    def over_down(block):
        return move(
            staged.at[block], down_in.at[block], flow_send.at[block], down_recv.at[block],
            device(z - 1, core, x),
        )

    def add(ref):
        total[...] += ref[...].astype(f32)

    def launch(shift, other, to_z, to_x, block):
        over_core(to_z, to_x, block).start()

    def work(shift, other, to_z, to_x, block):
        over_core(to_z, to_x, block).wait_recv()
        total[...] = own_ref[(to_z * 2 + core) * 2 + to_x].astype(f32) + core_in[block].astype(f32)
        along = True if other == 0 else core == 0
        if other == 0:
            @pl.when((core == 1) | (shift == 0))
            def _():
                over_x(to_z, block).wait_recv()
                add(x_in.at[to_z])
        if shift >= 0:
            @pl.when(along & (z > 0))
            def _():
                over_up(block).wait_recv()
                add(up_in.at[block])
        if shift <= 0:
            @pl.when(along & (z < height - 1))
            def _():
                over_down(block).wait_recv()
                add(down_in.at[block])
        if shift == 0 and other == 0:
            out_ref[...] = total[...].astype(out_ref.dtype)
        else:
            staged[block] = total[...].astype(staged.dtype)
            flow(shift, other, to_z, block, lambda copy: copy.start())

    def flow(shift, other, to_z, block, act):
        if other == 1 and shift == 0:
            act(over_x(to_z, block))
            return
        passing = over_up if shift > 0 else over_down
        if other == 0:
            act(passing(block))
            return

        @pl.when(core == 0)
        def _():
            act(passing(block))

        @pl.when(core == 1)
        def _():
            act(over_x(to_z, block))

    def settle(shift, other, to_z, to_x, block):
        over_core(to_z, to_x, block).wait_send()
        if not (shift == 0 and other == 0):
            flow(shift, other, to_z, block, lambda copy: copy.wait_send())

    each(launch)
    each(work)
    each(settle)


def scatter_sum(parts, height):
    vmem = pl.BlockSpec(memory_space=pltpu.VMEM)
    block = parts.shape[1:]
    dma = pltpu.SemaphoreType.DMA
    half = 2 * height
    return pl.pallas_call(
        lambda *refs: reduce_kernel(height, *refs),
        out_shape=jax.ShapeDtypeStruct(block, parts.dtype),
        in_specs=[vmem],
        out_specs=vmem,
        scratch_shapes=[
            pltpu.VMEM((half,) + block, parts.dtype),
            pltpu.VMEM((half,) + block, parts.dtype),
            pltpu.VMEM((half,) + block, parts.dtype),
            pltpu.VMEM((height,) + block, parts.dtype),
            pltpu.VMEM((half,) + block, parts.dtype),
            pltpu.VMEM(block, jnp.float32),
            dma((half,)), dma((half,)), dma((half,)), dma((half,)), dma((half,)), dma((height,)),
        ],
        compiler_params=pltpu.CompilerParams(
            collective_id=1, has_side_effects=True, vmem_limit_bytes=24 * 1024 * 1024
        ),
    )(parts)


def local_gather(tokens, cotangent, routes, mix_weights, gate_matrix, up_matrix, down_matrix):
    f32, bf16 = jnp.float32, jnp.bfloat16
    tok_count, features = tokens.shape
    top_count = routes.shape[1]
    height = lax.axis_size("expert") // 2
    devices = experts = lax.axis_size("expert") * lax.axis_size("dp")
    slot_most = min(5 * tok_count * top_count // (4 * experts), tok_count)
    rows = devices * slot_most
    mine = lax.axis_index("expert") * lax.axis_size("dp") + lax.axis_index("dp")
    named = jnp.concatenate([routes.astype(bf16), mix_weights], axis=1)
    named = jnp.pad(named, ((0, tok_count), (0, 128 - 2 * top_count)))
    packed = jnp.concatenate(
        [jnp.concatenate([tokens, cotangent], axis=0), named], axis=1
    )
    world = gather(packed, height)
    named = world[:, :tok_count, features : features + top_count] == mine.astype(bf16)
    heavy = world[:, :tok_count, features + top_count : features + 2 * top_count]
    weight = jnp.sum(jnp.where(named, heavy, 0).astype(f32), axis=2)
    hit = jnp.any(named, axis=2)
    ahead = (
        jnp.arange(tok_count)[:, None] < jnp.arange(tok_count)[None, :]
    ).astype(bf16)
    place = jnp.dot(hit.astype(bf16), ahead, preferred_element_type=f32).astype(jnp.int32)
    place = place + jnp.arange(devices, dtype=jnp.int32)[:, None] * slot_most
    place = jnp.where(hit, place, -1)
    place_both = jnp.concatenate([place, jnp.where(hit, place + rows, -1)], axis=1)
    place_both = place_both.reshape(devices * 2 * tok_count)
    pick = (jnp.arange(2 * rows, dtype=jnp.int32)[:, None] == place_both[None, :]).astype(bf16)
    flat = world.reshape(devices * 2 * tok_count, world.shape[2])[:, :features]
    row_both = jnp.dot(pick, flat, preferred_element_type=f32).astype(bf16)
    weight_both = jnp.pad(weight, ((0, 0), (0, tok_count))).reshape(-1)
    row_mix = jnp.sum(pick[:rows].astype(f32) * weight_both[None, :], axis=1).astype(bf16)
    token_partial, mix_partial, gate_grad, up_grad, down_grad = expert_backward(
        row_both[:rows], row_both[rows:], row_mix, gate_matrix, up_matrix, down_matrix, tiled=True
    )
    lane = (jnp.arange(128, dtype=jnp.int32)[None, :] == mine).astype(bf16)
    half = features // 2
    back = jnp.concatenate(
        [
            jnp.concatenate([token_partial[:, :half], token_partial[:, half:]], axis=0),
            jnp.pad(mix_partial[:, None] * lane, ((0, rows), (0, 0))),
        ],
        axis=1,
    )
    spread = lax.dot_general(
        pick, back, (((0,), (0,)), ((), ())), preferred_element_type=f32
    ).astype(bf16)
    home = scatter_sum(spread.reshape(devices, 2 * tok_count, half + 128), height)
    grad_tokens = jnp.concatenate([home[:tok_count, :half], home[tok_count:, :half]], axis=1)
    chosen = routes[:, :, None] == jnp.arange(experts, dtype=jnp.int32)[None, None, :]
    grad_mix = jnp.sum(
        jnp.where(chosen, home[:tok_count, None, half : half + experts].astype(f32), 0.0), axis=2
    )
    return (grad_tokens, grad_mix, gate_grad, up_grad, down_grad)


def solution(mesh):
    local = local_gather if mesh.shape["dp"] == 2 else local_exchange
    in_specs = (
        P(("groups", "expert", "dp"), None),
        P(("groups", "expert", "dp"), None),
        P(("groups", "expert", "dp"), None),
        P(("groups", "expert", "dp"), None),
        P(None, ("expert", "dp")),
        P(None, ("expert", "dp")),
        P(("expert", "dp"), None),
    )
    out_specs = (
        P(("groups", "expert", "dp"), None),
        P(("groups", "expert", "dp"), None),
        P(None, ("groups", "expert", "dp")),
        P(None, ("groups", "expert", "dp")),
        P(("groups", "expert", "dp"), None),
    )
    return jax.shard_map(local, mesh=mesh, in_specs=in_specs, out_specs=out_specs, check_vma=False)
```
